32 devices in a mesh: river: 4 (over x, core), hours: 8 (over z, y).
Axes of the slice: x: 2, y: 2, z: 4, core: 2. Of those that a mesh axis runs over, the one named last changes fastest.
Arguments:
- release: float32 [40, 128, 512], P('river', 'hours'), may hold values from 0 to 1
- storage_dual: float32 [40, 128, 512], P('river', 'hours'), may hold values from -3 to 3
- demand_dual: float32 [128, 512], P('hours'), may hold values from -1 to 0
- cost: float32 [40, 128, 512], P('river', 'hours'), may hold values from -1.8 to 1.8
- inflow: float32 [40, 128, 512], P('river', 'hours'), may hold values from 0 to 1.2
- demand: float32 [128, 512], P('hours'), may hold values from 2.2135944 to 4.110961
- storage_start: float32 [40], P('river'), may hold values from -0.5 to 0.5
- storage_low: float32 [40], P('river'), may hold values from -2 to -0.5
- storage_high: float32 [40], P('river'), may hold values from 0.5 to 2
- release_cap: float32 [40], P('river'), may hold values from 0.5 to 1.5
- efficiency: float32 [40], P('river'), may hold values from 0.5 to 1.5
- downstream: int32 [40], P('river'), may hold values from -1 to 39, as said below
- travel_delay: int32 [40], P('river'), may hold values from 1 to 6
Outputs:
- release_new: float32 [40, 128, 512], P('river', 'hours')
- storage_dual_new: float32 [40, 128, 512], P('river', 'hours')
- demand_dual_new: float32 [128, 512], P('hours')
- storage_excess: float32 [40, 128, 512], P('river', 'hours')
The draws below stay inside these ranges and needn't reach their ends.
Inputs may be any that keep to these rules, and one draw needn't show every extreme that they name: Each reservoir's downstream index is -1 or lies 1 to 10 positions after its own index.
All inputs are finite; a program needn't handle non-finite values.
Results may differ from the reference program's by a relative error of at most 0.00013.
Values sent between devices are 32-bit elements; how exact they have to be, the bound alone decides.
No kernel may reach another device: no remote copies, remote signals or barrier semaphores. Data moves between devices by JAX's collectives and lax.ppermute only.
A program may use at most 64 MiB of HBM per device.

```python
import math
import jax
import jax.numpy as jnp
from jax import lax

RES_DEV = 10
DMAX = 6
SC = 512
RES = 40
HOURS = 128


def draw_downstream(key, part):
    position = jnp.arange(RES, dtype=jnp.int32)
    offset = jax.random.randint(key, (RES,), 1, RES_DEV + 1, dtype=jnp.int32)
    offset = jnp.where(position % RES_DEV >= RES_DEV - 2, 1, offset)
    target = position + offset
    return jnp.where(target < RES, target, -1).astype(jnp.int32)


def plant(drawn, own_key, least, largest):
    extent = drawn.shape
    spot = [jax.random.randint(jax.random.fold_in(own_key, axis), (), 0, extent[axis]) for axis in range(len(extent))]
    drawn = drawn.at[tuple(spot)].set(least)
    longest = extent.index(max(extent))
    spot[longest] = (spot[longest] + 1) % extent[longest]
    return drawn.at[tuple(spot)].set(largest)


def steps_of(own_key, dims, cuts, low, high):
    loudness, own = 1.0, jax.random.fold_in(own_key, 6)
    for dim, shards_of in cuts:
        heights = jnp.exp(jax.random.uniform(jax.random.fold_in(own, dim), (shards_of,), jnp.float32, low / len(cuts), high / len(cuts)))
        loudness = loudness * jnp.repeat(heights, dims[dim] // shards_of).reshape([-1 if axis == dim else 1 for axis in range(len(dims))])
    return loudness


def normal_values(stream_key, extent, width, most, pieces=(), held_as=jnp.bfloat16):
    array = jax.random.normal(stream_key, extent, jnp.float32) * width
    if len(pieces) > 0:
        array = steps_of(stream_key, extent, pieces, -0.22, 0.18) * array
    return jnp.clip(array, min=-most, max=most).astype(held_as)


def setup_inputs(seed: int = 0) -> dict:
    splits = jax.random.split(jax.random.key(seed), 14)
    return {
        "release": jnp.clip(1.0 * jax.random.uniform(splits[0], (RES, HOURS, SC), jnp.float32) ** steps_of(splits[0], (RES, HOURS, SC), ((0, 4), (1, 8)), -0.2, 0.2), 0.0, 1.0),
        "storage_dual": normal_values(splits[1], (RES, HOURS, SC), 0.5, 3.0, ((0, 4), (1, 8)), jnp.float32),
        "demand_dual": jnp.clip(-1.0 + 1.0 * jax.random.uniform(splits[2], (HOURS, SC), jnp.float32) ** steps_of(splits[2], (HOURS, SC), ((0, 8),), -0.2, 0.2), -1.0, 0.0),
        "cost": normal_values(splits[3], (RES, HOURS, SC), 0.3, 1.8, ((0, 4), (1, 8)), jnp.float32),
        "inflow": jnp.clip(1.2 * jax.random.uniform(splits[4], (RES, HOURS, SC), jnp.float32) ** steps_of(splits[4], (RES, HOURS, SC), ((0, 4), (1, 8)), -0.2, 0.2), 0.0, 1.2),
        "demand": jnp.clip(2.2135944 + 1.8973665 * jax.random.uniform(splits[5], (HOURS, SC), jnp.float32) ** steps_of(splits[5], (HOURS, SC), ((0, 8),), -0.2, 0.2), 2.2135944, 4.110961),
        "storage_start": jnp.clip(jax.random.uniform(splits[6], (RES,), jnp.float32, -0.5, 0.5) * steps_of(splits[6], (RES,), ((0, 4),), -0.4, 0.0), -0.5, 0.5),
        "storage_low": jnp.clip(-2.0 + 1.5 * jax.random.uniform(splits[7], (RES,), jnp.float32) ** steps_of(splits[7], (RES,), ((0, 4),), -0.2, 0.2), -2.0, -0.5),
        "storage_high": jnp.clip(0.5 + 1.5 * jax.random.uniform(splits[8], (RES,), jnp.float32) ** steps_of(splits[8], (RES,), ((0, 4),), -0.2, 0.2), 0.5, 2.0),
        "release_cap": jnp.clip(0.5 + 1.0 * jax.random.uniform(splits[9], (RES,), jnp.float32) ** steps_of(splits[9], (RES,), ((0, 4),), -0.2, 0.2), 0.5, 1.5),
        "efficiency": jnp.clip(0.5 + 1.0 * jax.random.uniform(splits[10], (RES,), jnp.float32) ** steps_of(splits[10], (RES,), ((0, 4),), -0.2, 0.2), 0.5, 1.5),
        "downstream": draw_downstream(jax.random.fold_in(splits[13], 71), 0),
        "travel_delay": plant(jax.random.randint(splits[12], (RES,), 1, DMAX + 1), jax.random.fold_in(splits[12], 1), 1, DMAX).astype(jnp.int32),
    }


primal_step = 1.0
dual_step = 0.1

def reference(release, storage_dual, demand_dual, cost, inflow, demand, storage_start, storage_low, storage_high, release_cap, efficiency, downstream, travel_delay):
    scale_time = 1.0 / HOURS
    scale_sum = 1.0 / math.sqrt(RES)
    sink_index = jnp.where(downstream < 0, RES, downstream).astype(jnp.int32)
    suffix = jnp.flip(jnp.cumsum(jnp.flip(storage_dual, 1), 1), 1)
    padded = jnp.concatenate([suffix, jnp.zeros((1, HOURS, SC), jnp.float32)], 0)
    at_sink = padded[sink_index]
    later_duals = jnp.zeros((RES, HOURS, SC), jnp.float32)
    for lag_hours in range(1, DMAX + 1):
        shifted = jnp.concatenate([at_sink[:, lag_hours:], jnp.zeros((RES, lag_hours, SC), jnp.float32)], 1)
        later_duals = later_duals + jnp.where((travel_delay == lag_hours)[:, None, None], shifted, 0.0)
    gradient = cost + scale_time * (later_duals - suffix) + scale_sum * efficiency[:, None, None] * demand_dual[None]
    release_new = jnp.clip(release - primal_step * gradient, 0.0, release_cap[:, None, None])
    extrapolated = 2.0 * release_new - release
    delayed = jnp.zeros((RES, HOURS, SC), jnp.float32)
    for lag_hours in range(1, DMAX + 1):
        shifted = jnp.concatenate([jnp.zeros((RES, lag_hours, SC), jnp.float32), extrapolated[:, :HOURS - lag_hours]], 1)
        delayed = delayed + jnp.where((travel_delay == lag_hours)[:, None, None], shifted, 0.0)
    routed = jax.ops.segment_sum(delayed, sink_index, num_segments=RES + 1)[:RES]
    storage = storage_start[:, None, None] + scale_time * jnp.cumsum(inflow + routed - extrapolated, 1)
    lower_bound = storage_low[:, None, None]
    upper_bound = storage_high[:, None, None]
    storage_dual_new = storage_dual + dual_step * storage - dual_step * jnp.clip(storage_dual / dual_step + storage, lower_bound, upper_bound)
    storage_excess = storage - jnp.clip(storage, lower_bound, upper_bound)
    supplied = lax.optimization_barrier(jnp.sum(scale_sum * efficiency[:, None, None] * extrapolated, 0))
    demand_dual_new = jnp.minimum(demand_dual + dual_step * (supplied - demand), 0.0)
    return (release_new, storage_dual_new, demand_dual_new, storage_excess)
```

```python
import functools
import math

import jax
import jax.numpy as jnp
from jax import lax
from jax.experimental import pallas as pl
from jax.experimental.pallas import tpu as pltpu
from jax.sharding import PartitionSpec as P

DMAX = 6
RIM = 8

primal_step = 1.0
dual_step = 0.1


def scan_rows(block, reverse):
    rows, lanes = block.shape
    place = lax.broadcasted_iota(jnp.int32, (8, lanes), 0)
    tiles = [block[k : k + 8] for k in range(0, rows, 8)]
    order = range(len(tiles) - 1, -1, -1) if reverse else range(len(tiles))
    carry = None
    for k in order:
        tile = tiles[k]
        for step in (1, 2, 4):
            moved = pltpu.roll(tile, 8 - step if reverse else step, 0)
            keep = place < 8 - step if reverse else place >= step
            tile = tile + jnp.where(keep, moved, 0.0)
        if carry is not None:
            tile = tile + carry
        tiles[k] = tile
        carry = tile[0:1] if reverse else tile[7:8]
    return jnp.concatenate(tiles, 0), carry


def sink_of(down_ref, j, count):
    down = down_ref[j]
    base = lax.axis_index("river") * count
    return jnp.where(down < 0, 2 * count, down - base)


def turned(tiles, amount):
    return [pltpu.roll(tile, amount, 0) for tile in tiles]


def totals_kernel(sd_ref, total_ref):
    for i in range(sd_ref.shape[0]):
        total_ref[i : i + 1] = jnp.sum(sd_ref[i], 0, keepdims=True)


def ahead_kernel(scale_time, scale_sum, down_ref, delay_ref, eff_ref, sd_ref, next_ref, rel_ref, cost_ref, dual_ref, q_ref, w_ref, sums_ref):
    count, hours, lanes = sd_ref.shape
    for i in range(2 * count):
        ref, k = (sd_ref, i) if i < count else (next_ref, i - count)
        sums_ref[i] = scan_rows(ref[k], True)[0]
    sums_ref[2 * count] = jnp.zeros((hours, lanes), jnp.float32)
    dual = dual_ref[...]
    place = lax.broadcasted_iota(jnp.int32, (RIM, lanes), 0)
    for j in range(count):
        lag = delay_ref[j]
        sink = sums_ref[sink_of(down_ref, j, count)]
        inside = place < RIM - lag
        tiles = turned([sink[k : k + RIM] for k in range(0, hours, RIM)], RIM - lag)
        w_ref[j] = jnp.where(inside, 0.0, tiles[0] - sink[0:1])
        tiles.append(jnp.zeros((RIM, lanes), jnp.float32))
        later = jnp.concatenate([jnp.where(inside, tiles[k], tiles[k + 1]) for k in range(hours // RIM)], 0)
        gradient = cost_ref[j] + scale_time * (later - sums_ref[j]) + scale_sum * eff_ref[j] * dual
        q_ref[j] = rel_ref[j] - primal_step * gradient


def release_kernel(scale_time, scale_sum, down_ref, delay_ref, eff_ref, cap_ref, q_ref, w_ref, own_ref, next_ref, rel_ref, inflow_ref, new_ref, own_out, next_out, tot_own, tot_next, power_ref, acc, tot):
    count, hours, lanes = q_ref.shape
    for i in range(count):
        tot[i] = own_ref[i : i + 1]
        tot[count + i] = next_ref[i : i + 1]
    tot[2 * count] = jnp.zeros((1, lanes), jnp.float32)
    lags = [delay_ref[j] for j in range(count)]
    sinks = [sink_of(down_ref, j, count) for j in range(count)]
    shifts = [tot[sinks[j]] - tot[j] for j in range(count)]
    acc[...] = jnp.zeros_like(acc)
    tot[...] = jnp.zeros_like(tot)
    power = jnp.zeros((hours, lanes), jnp.float32)
    place = lax.broadcasted_iota(jnp.int32, (RIM, lanes), 0)
    zeros = jnp.zeros((RIM, lanes), jnp.float32)
    for j in range(count):
        later = jnp.concatenate([jnp.zeros((hours - RIM, lanes), jnp.float32), w_ref[j]], 0) + shifts[j]
        release = rel_ref[j]
        new = jnp.clip(q_ref[j] - (primal_step * scale_time) * later, 0.0, cap_ref[j])
        new_ref[j] = new
        extra = 2.0 * new - release
        power = power + (scale_sum * eff_ref[j]) * extra
        sums, total = scan_rows(extra, False)
        arrived = place >= lags[j]
        tiles = [zeros] + turned([sums[k : k + RIM] for k in range(0, hours, RIM)], lags[j])
        window = [jnp.where(arrived, tiles[k + 1], tiles[k]) for k in range(hours // RIM)]
        window.append(jnp.where(arrived, 0.0, tiles[-1] - total))
        acc[sinks[j]] = acc[sinks[j]] + jnp.concatenate(window, 0)
        tot[sinks[j]] = tot[sinks[j]] + total
        local, change = scan_rows(inflow_ref[j] - extra, False)
        acc[j, 0:hours] = acc[j, 0:hours] + local
        tot[j] = tot[j] + change
    own_out[...] = acc[0:count]
    next_out[...] = acc[count : 2 * count]
    for i in range(count):
        tot_own[i : i + 1] = tot[i]
        tot_next[i : i + 1] = tot[count + i]
    power_ref[...] = power


def storage_kernel(scale_time, start_ref, low_ref, high_ref, mine_ref, came_ref, rim_ref, off_ref, sd_ref, power_ref, dual_ref, demand_ref, sd_out, excess_out, dual_out):
    count, hours, lanes = sd_ref.shape
    for i in range(count):
        change = mine_ref[i, 0:hours] + came_ref[i, 0:hours] + off_ref[i : i + 1]
        rim = jnp.concatenate([rim_ref[i], jnp.zeros((hours - RIM, lanes), jnp.float32)], 0)
        storage = start_ref[i] + scale_time * (change + rim)
        low, high = low_ref[i], high_ref[i]
        dual = sd_ref[i]
        sd_out[i] = dual + dual_step * storage - dual_step * jnp.clip(dual / dual_step + storage, low, high)
        excess_out[i] = storage - jnp.clip(storage, low, high)
    dual_out[...] = jnp.minimum(dual_ref[...] + dual_step * (power_ref[...] - demand_ref[...]), 0.0)


def passed_along(block, axis, distance):
    devices = range(lax.axis_size(axis))
    route = [(i - distance, i) for i in devices if i - distance in devices]
    return lax.ppermute(block, axis, route)


def swapped(block, axis, bit):
    return lax.ppermute(block, axis, [(i, i ^ bit) for i in range(lax.axis_size(axis))])


def offsets(total, axis, reverse):
    count, place = lax.axis_size(axis), lax.axis_index(axis)
    result = jnp.zeros_like(total)
    bit = 1
    while bit < count:
        other = swapped(total, axis, bit)
        low = (place & bit) == 0
        result = result + jnp.where(low if reverse else ~low, other, 0.0)
        total = total + other
        bit *= 2
    return result


def all_summed(part, axis):
    count = lax.axis_size(axis)
    bit = 1
    while bit < count:
        part = part + swapped(part, axis, bit)
        bit *= 2
    return part


SMEM = pl.BlockSpec(memory_space=pltpu.SMEM)
VMEM = pl.BlockSpec(memory_space=pltpu.VMEM)


def call(body, smem, vmem, shapes, scratch):
    return pl.pallas_call(
        body,
        out_shape=[jax.ShapeDtypeStruct(s, jnp.float32) for s in shapes],
        in_specs=[SMEM] * len(smem) + [VMEM] * len(vmem),
        out_specs=[VMEM] * len(shapes),
        scratch_shapes=[pltpu.VMEM(s, jnp.float32) for s in scratch],
        compiler_params=pltpu.CompilerParams(vmem_limit_bytes=32 * 1024 * 1024),
    )(*smem, *vmem)


def shards(
    release,
    storage_dual,
    demand_dual,
    cost,
    inflow,
    demand,
    storage_start,
    storage_low,
    storage_high,
    release_cap,
    efficiency,
    downstream,
    travel_delay,
):
    count, hours, lanes = release.shape
    scale_time = 1.0 / (hours * lax.axis_size("hours"))
    scale_sum = 1.0 / math.sqrt(count * lax.axis_size("river"))
    slab, flat, rim = (count, hours, lanes), (count, lanes), (count, RIM, lanes)
    wide = (count, hours + RIM, lanes)

    sd_next = passed_along(storage_dual, "river", -1)
    (total,) = call(totals_kernel, (), (storage_dual,), [flat], [])
    off_own = offsets(total, "hours", True)
    off_next = passed_along(off_own, "river", -1)
    q, w = call(
        functools.partial(ahead_kernel, scale_time, scale_sum),
        (downstream, travel_delay, efficiency),
        (storage_dual, sd_next, release, cost, demand_dual),
        [slab, rim],
        [(2 * count + 1, hours, lanes)],
    )
    w = passed_along(w, "hours", -1)
    release_new, mine, theirs, tot_own, tot_next, power = call(
        functools.partial(release_kernel, scale_time, scale_sum),
        (downstream, travel_delay, efficiency, release_cap),
        (q, w, off_own, off_next, release, inflow),
        [slab, wide, wide, flat, flat, (hours, lanes)],
        [(2 * count + 1, hours + RIM, lanes), (2 * count + 1, 1, lanes)],
    )
    came = passed_along(theirs, "river", 1)
    tot_came = passed_along(tot_next, "river", 1)
    off = offsets(tot_own + tot_came, "hours", False)
    edge = passed_along(mine[:, hours:] + came[:, hours:], "hours", 1)
    supplied = all_summed(power, "river")
    storage_dual_new, storage_excess, demand_dual_new = call(
        functools.partial(storage_kernel, scale_time),
        (storage_start, storage_low, storage_high),
        (mine, came, edge, off, storage_dual, supplied, demand_dual, demand),
        [slab, slab, (hours, lanes)],
        [],
    )
    return (release_new, storage_dual_new, demand_dual_new, storage_excess)


def solution(mesh):
    field, flat, row = P("river", "hours", None), P("hours", None), P("river")
    return jax.shard_map(
        shards,
        mesh=mesh,
        in_specs=(field, field, flat, field, field, flat) + (row,) * 7,
        out_specs=(field, field, flat, field),
        check_vma=False,
    )
```

```python
import functools
import math

import jax
import jax.numpy as jnp
from jax import lax
from jax.experimental import pallas as pl
from jax.experimental.pallas import tpu as pltpu
from jax.sharding import PartitionSpec as P

DMAX = 6
RIM = 8

primal_step = 1.0
dual_step = 0.1


def scan_rows(block, reverse):
    rows, lanes = block.shape
    place = lax.broadcasted_iota(jnp.int32, (8, lanes), 0)
    tiles = [block[k : k + 8] for k in range(0, rows, 8)]
    order = range(len(tiles) - 1, -1, -1) if reverse else range(len(tiles))
    carry = None
    for k in order:
        tile = tiles[k]
        for step in (1, 2, 4):
            moved = pltpu.roll(tile, 8 - step if reverse else step, 0)
            keep = place < 8 - step if reverse else place >= step
            tile = tile + jnp.where(keep, moved, 0.0)
        if carry is not None:
            tile = tile + carry
        tiles[k] = tile
        carry = tile[0:1] if reverse else tile[7:8]
    return jnp.concatenate(tiles, 0), carry


def sink_of(down_ref, j, count):
    down = down_ref[j]
    base = lax.axis_index("river") * count
    return jnp.where(down < 0, 2 * count, down - base)


def turned(tiles, amount):
    return [pltpu.roll(tile, amount, 0) for tile in tiles]


def totals_kernel(sd_ref, total_ref):
    for i in range(sd_ref.shape[0]):
        total_ref[i : i + 1] = jnp.sum(sd_ref[i], 0, keepdims=True)


def price_kernel(scale_sum, eff_hbm, cap_hbm, start_hbm, low_hbm, high_hbm, rel_ref, cost_ref, dual_ref, base_ref, rows_ref, scalars, sems):
    count, hours, lanes = base_ref.shape
    small = (eff_hbm, cap_hbm, start_hbm, low_hbm, high_hbm)
    copies = [pltpu.make_async_copy(ref, scalars.at[k], sems.at[k]) for k, ref in enumerate(small)]
    for copy in copies:
        copy.start()
    for copy in copies:
        copy.wait()
    dual = dual_ref[...]
    for j in range(count):
        for k in range(5):
            at = k * count + j
            rows_ref[at : at + 1] = jnp.full((1, lanes), scalars[k, j], jnp.float32)
        base_ref[j] = rel_ref[j] - primal_step * (cost_ref[j] + (scale_sum * scalars[0, j]) * dual)


def stock_kernel(inflow_ref, stock_ref):
    for j in range(inflow_ref.shape[0]):
        stock_ref[j] = scan_rows(inflow_ref[j], False)[0]


def copy_kernel(in_ref, out_ref):
    out_ref[...] = in_ref[...]


def route_kernel(down_ref, delay_ref, sd_ref, next_ref, lead_ref, w_ref, sums_ref):
    count, hours, lanes = sd_ref.shape
    for i in range(2 * count):
        ref, k = (sd_ref, i) if i < count else (next_ref, i - count)
        sums_ref[i] = scan_rows(ref[k], True)[0]
    sums_ref[2 * count] = jnp.zeros((hours, lanes), jnp.float32)
    place = lax.broadcasted_iota(jnp.int32, (RIM, lanes), 0)
    for j in range(count):
        lag = delay_ref[j]
        sink = sums_ref[sink_of(down_ref, j, count)]
        inside = place < RIM - lag
        tiles = turned([sink[k : k + RIM] for k in range(0, hours, RIM)], RIM - lag)
        w_ref[j] = jnp.where(inside, 0.0, tiles[0] - sink[0:1])
        tiles.append(jnp.zeros((RIM, lanes), jnp.float32))
        later = jnp.concatenate([jnp.where(inside, tiles[k], tiles[k + 1]) for k in range(hours // RIM)], 0)
        lead_ref[j] = later - sums_ref[j]


def release_kernel(scale_time, scale_sum, down_ref, delay_ref, rows_ref, base_ref, lead_ref, w_ref, own_ref, next_ref, rel_ref, stock_ref, new_hbm, mine_ref, theirs_ref, tots_ref, power_ref, tot, new_ref, sems):
    count, hours, lanes = base_ref.shape
    for i in range(count):
        tot[i] = own_ref[i : i + 1]
        tot[count + i] = next_ref[i : i + 1]
    tot[2 * count] = jnp.zeros((1, lanes), jnp.float32)
    lags = [delay_ref[j] for j in range(count)]
    sinks = [sink_of(down_ref, j, count) for j in range(count)]
    shifts = [tot[sinks[j]] - tot[j] for j in range(count)]
    tot[...] = jnp.zeros_like(tot)
    mine_ref[...] = jnp.zeros_like(mine_ref)
    theirs_ref[...] = jnp.zeros_like(theirs_ref)
    power = jnp.zeros((hours, lanes), jnp.float32)
    place = lax.broadcasted_iota(jnp.int32, (RIM, lanes), 0)
    zeros = jnp.zeros((RIM, lanes), jnp.float32)
    more = lax.axis_index("hours") < lax.axis_size("hours") - 1
    copies = [pltpu.make_async_copy(new_ref.at[j], new_hbm.at[j], sems.at[j]) for j in range(count)]
    for j in range(count):
        rim = jnp.where(more, w_ref[j], 0.0)
        later = lead_ref[j] + (jnp.concatenate([jnp.zeros((hours - RIM, lanes), jnp.float32), rim], 0) + shifts[j])
        release = rel_ref[j]
        new = jnp.clip(base_ref[j] - (primal_step * scale_time) * later, 0.0, rows_ref[count + j : count + j + 1])
        new_ref[j] = new
        copies[j].start()
        extra = 2.0 * new - release
        power = power + (scale_sum * rows_ref[j : j + 1]) * extra
        sums, total = scan_rows(extra, False)
        arrived = place >= lags[j]
        tiles = [zeros] + turned([sums[k : k + RIM] for k in range(0, hours, RIM)], lags[j])
        window = [jnp.where(arrived, tiles[k + 1], tiles[k]) for k in range(hours // RIM)]
        window.append(jnp.where(arrived, 0.0, tiles[-1] - total))
        window = jnp.concatenate(window, 0)

        @pl.when(sinks[j] < count)
        def _():
            mine_ref[sinks[j]] = mine_ref[sinks[j]] + window

        @pl.when((sinks[j] >= count) & (sinks[j] < 2 * count))
        def _():
            theirs_ref[sinks[j] - count] = theirs_ref[sinks[j] - count] + window

        tot[sinks[j]] = tot[sinks[j]] + total
        local = stock_ref[j] - sums
        mine_ref[j, 0:hours] = mine_ref[j, 0:hours] + local
        tot[j] = tot[j] + local[hours - 1 : hours]
    for i in range(2 * count):
        tots_ref[i : i + 1] = tot[i]
    power_ref[...] = power
    for copy in copies:
        copy.wait()


def storage_kernel(scale_time, rows_ref, mine_ref, came_ref, rim_ref, off_ref, offcame_ref, sd_ref, power_ref, dual_ref, demand_ref, sd_hbm, excess_hbm, dual_out, sd_out, excess_out, sems):
    count, hours, lanes = sd_ref.shape
    earlier = lax.axis_index("hours") > 0
    copies = [[pltpu.make_async_copy(src.at[i], dst.at[i], sems.at[k, i]) for i in range(count)] for k, (src, dst) in enumerate(((sd_out, sd_hbm), (excess_out, excess_hbm)))]
    for i in range(count):
        row = [rows_ref[k * count + i : k * count + i + 1] for k in range(5)]
        change = mine_ref[i, 0:hours] + came_ref[i, 0:hours] + (off_ref[i : i + 1] + offcame_ref[i : i + 1])
        rim = jnp.concatenate([jnp.where(earlier, rim_ref[i], 0.0), jnp.zeros((hours - RIM, lanes), jnp.float32)], 0)
        storage = row[2] + scale_time * (change + rim)
        low, high = row[3], row[4]
        dual = sd_ref[i]
        sd_out[i] = dual + dual_step * storage - dual_step * jnp.clip(dual / dual_step + storage, low, high)
        copies[0][i].start()
        excess_out[i] = storage - jnp.clip(storage, low, high)
        copies[1][i].start()
    dual_out[...] = jnp.minimum(dual_ref[...] + dual_step * (power_ref[...] - demand_ref[...]), 0.0)
    for i in range(count):
        for k in range(2):
            copies[k][i].wait()


def passed_along(block, axis, distance):
    count = lax.axis_size(axis)
    return lax.ppermute(block, axis, [(i, (i + distance) % count) for i in range(count)])


def swapped(block, axis, bit):
    return lax.ppermute(block, axis, [(i, i ^ bit) for i in range(lax.axis_size(axis))])


def offsets(total, axis, reverse, beside):
    count, place = lax.axis_size(axis), lax.axis_index(axis)
    result = jnp.zeros_like(total)
    for step in range((count - 1).bit_length()):
        bit = 1 << step
        other = swapped(total, axis, bit)
        if step < len(beside) and beside[step]:
            other, *_ = lax.optimization_barrier((other, *beside[step]))
        low = (place & bit) == 0
        result = result + jnp.where(low if reverse else ~low, other, 0.0)
        total = total + other
    return result


def all_summed(part, axis):
    count, first = lax.axis_size(axis), None
    for step in range((count - 1).bit_length()):
        part = part + swapped(part, axis, 1 << step)
        first = part if first is None else first
    return part, first


SMEM = pl.BlockSpec(memory_space=pltpu.SMEM)
VMEM = pl.BlockSpec(memory_space=pltpu.VMEM)
HBM = pl.BlockSpec(memory_space=pltpu.HBM)


def call(body, ins, outs, scratch):
    return pl.pallas_call(
        body,
        out_shape=[jax.ShapeDtypeStruct(shape, jnp.float32) for _, shape in outs],
        in_specs=[spec for spec, _ in ins],
        out_specs=[spec for spec, _ in outs],
        scratch_shapes=[pltpu.VMEM(entry, jnp.float32) if isinstance(entry, tuple) else entry for entry in scratch],
        compiler_params=pltpu.CompilerParams(vmem_limit_bytes=32 * 1024 * 1024),
    )(*(array for _, array in ins))


def shards(
    release,
    storage_dual,
    demand_dual,
    cost,
    inflow,
    demand,
    storage_start,
    storage_low,
    storage_high,
    release_cap,
    efficiency,
    downstream,
    travel_delay,
):
    count, hours, lanes = release.shape
    scale_time = 1.0 / (hours * lax.axis_size("hours"))
    scale_sum = 1.0 / math.sqrt(count * lax.axis_size("river"))
    slab, flat, rim = (count, hours, lanes), (count, lanes), (count, RIM, lanes)
    wide = (count, hours + RIM, lanes)
    dma = pltpu.SemaphoreType.DMA

    (total,) = call(totals_kernel, [(VMEM, storage_dual)], [(VMEM, flat)], [])
    sd = storage_dual
    (sd_sent,) = call(copy_kernel, [(VMEM, lax.optimization_barrier((storage_dual, total))[0])], [(VMEM, slab)], [])
    sd_next = passed_along(sd_sent, "river", -1)
    base, rows = call(
        functools.partial(price_kernel, scale_sum),
        [(HBM, a) for a in (efficiency, release_cap, storage_start, storage_low, storage_high)] + [(VMEM, a) for a in (release, cost, demand_dual)],
        [(VMEM, slab), (VMEM, (5 * count, lanes))],
        [pltpu.SMEM((5, count), jnp.float32), dma((5,))],
    )
    (stock,) = call(stock_kernel, [(VMEM, inflow)], [(VMEM, slab)], [])
    lead, w = call(
        route_kernel,
        [(SMEM, downstream), (SMEM, travel_delay), (VMEM, sd), (VMEM, sd_next)],
        [(VMEM, slab), (VMEM, rim)],
        [(2 * count + 1, hours, lanes)],
    )
    off_own = offsets(total, "hours", True, [(base, rows), (lead, w), (stock,)])
    off_next = passed_along(off_own, "river", -1)
    w = passed_along(w, "hours", -1)
    release_new, mine, theirs, tots, power = call(
        functools.partial(release_kernel, scale_time, scale_sum),
        [(SMEM, downstream), (SMEM, travel_delay)] + [(VMEM, a) for a in (rows, base, lead, w, off_own, off_next, release, stock)],
        [(HBM, slab), (VMEM, wide), (VMEM, wide), (VMEM, (2 * count, lanes)), (VMEM, (hours, lanes))],
        [(2 * count + 1, 1, lanes), slab, dma((count,))],
    )
    came = passed_along(theirs, "river", 1)
    late = mine[:, hours:] + came[:, hours:]
    supplied, first = all_summed(power, "river")
    edge = passed_along(late, "hours", 1)
    off = offsets(tots, "hours", False, [(first,), (late,)])
    off_came = passed_along(off[count:], "river", 1)
    storage_dual_new, storage_excess, demand_dual_new = call(
        functools.partial(storage_kernel, scale_time),
        [(VMEM, a) for a in (rows, mine, came, edge, off[:count], off_came, sd, supplied, demand_dual, demand)],
        [(HBM, slab), (HBM, slab), (VMEM, (hours, lanes))],
        [slab, slab, dma((2, count))],
    )
    return (release_new, storage_dual_new, demand_dual_new, storage_excess)


def solution(mesh):
    field, flat, row = P("river", "hours", None), P("hours", None), P("river")
    return jax.shard_map(
        shards,
        mesh=mesh,
        in_specs=(field, field, flat, field, field, flat) + (row,) * 7,
        out_specs=(field, field, flat, field),
        check_vma=False,
    )
```

```python
import functools
import math

import jax
import jax.numpy as jnp
from jax import lax
from jax.experimental import pallas as pl
from jax.experimental.pallas import tpu as pltpu
from jax.sharding import PartitionSpec as P

DMAX = 6
RIM = 8
EDGE = DMAX - 1

primal_step = 1.0
dual_step = 0.1


def scan_rows(block, reverse):
    rows, lanes = block.shape
    place = lax.broadcasted_iota(jnp.int32, (8, lanes), 0)
    tiles = [block[k : k + 8] for k in range(0, rows, 8)]
    order = range(len(tiles) - 1, -1, -1) if reverse else range(len(tiles))
    carry = None
    for k in order:
        tile = tiles[k]
        for step in (1, 2, 4):
            moved = pltpu.roll(tile, 8 - step if reverse else step, 0)
            keep = place < 8 - step if reverse else place >= step
            tile = tile + jnp.where(keep, moved, 0.0)
        if carry is not None:
            tile = tile + carry
        tiles[k] = tile
        carry = tile[0:1] if reverse else tile[7:8]
    return jnp.concatenate(tiles, 0), carry


def sink_of(down_ref, j, count):
    down = down_ref[j]
    base = lax.axis_index("river") * count
    return jnp.where(down < 0, 2 * count, down - base)


def turned(tiles, amount):
    return [pltpu.roll(tile, amount, 0) for tile in tiles]


def totals_kernel(sd_ref, total_ref):
    for i in range(sd_ref.shape[0]):
        total_ref[i : i + 1] = jnp.sum(sd_ref[i], 0, keepdims=True)


def price_kernel(scale_sum, eff_hbm, cap_hbm, start_hbm, low_hbm, high_hbm, rel_ref, cost_ref, dual_ref, base_ref, rows_ref, scalars, sems):
    count, hours, lanes = base_ref.shape
    small = (eff_hbm, cap_hbm, start_hbm, low_hbm, high_hbm)
    copies = [pltpu.make_async_copy(ref, scalars.at[k], sems.at[k]) for k, ref in enumerate(small)]
    for copy in copies:
        copy.start()
    for copy in copies:
        copy.wait()
    dual = dual_ref[...]
    for j in range(count):
        for k in range(5):
            at = k * count + j
            rows_ref[at : at + 1] = jnp.full((1, lanes), scalars[k, j], jnp.float32)
        base_ref[j] = rel_ref[j] - primal_step * (cost_ref[j] + (scale_sum * scalars[0, j]) * dual)


def stock_kernel(inflow_ref, stock_ref):
    for j in range(inflow_ref.shape[0]):
        stock_ref[j] = scan_rows(inflow_ref[j], False)[0]


def copy_kernel(in_ref, out_ref):
    out_ref[...] = in_ref[...]


def route_kernel(down_ref, delay_ref, sd_ref, next_ref, lead_ref, w_ref, sums_ref):
    count, hours, lanes = sd_ref.shape
    for i in range(2 * count):
        ref, k = (sd_ref, i) if i < count else (next_ref, i - count)
        sums_ref[i] = scan_rows(ref[k], True)[0]
    sums_ref[2 * count] = jnp.zeros((hours, lanes), jnp.float32)
    place = lax.broadcasted_iota(jnp.int32, (RIM, lanes), 0)
    for j in range(count):
        lag = delay_ref[j]
        sink = sums_ref[sink_of(down_ref, j, count)]
        inside = place < RIM - lag
        tiles = turned([sink[k : k + RIM] for k in range(0, hours, RIM)], RIM - lag)
        w_ref[EDGE * j : EDGE * (j + 1)] = jnp.where(inside, 0.0, tiles[0] - sink[0:1])[RIM - EDGE :]
        tiles.append(jnp.zeros((RIM, lanes), jnp.float32))
        later = jnp.concatenate([jnp.where(inside, tiles[k], tiles[k + 1]) for k in range(hours // RIM)], 0)
        lead_ref[j] = later - sums_ref[j]


def release_kernel(scale_time, scale_sum, down_ref, delay_ref, rows_ref, base_ref, lead_ref, w_ref, own_ref, next_ref, rel_ref, stock_ref, new_hbm, mine_ref, theirs_ref, tots_ref, power_ref, tot, new_ref, extra_ref, late_ref, sems):
    count, hours, lanes = base_ref.shape
    for i in range(count):
        tot[i] = own_ref[i : i + 1]
        tot[count + i] = next_ref[i : i + 1]
    tot[2 * count] = jnp.zeros((1, lanes), jnp.float32)
    sinks = [sink_of(down_ref, j, count) for j in range(count)]
    shifts = [tot[sinks[j]] - tot[j] for j in range(count)]
    tot[...] = jnp.zeros_like(tot)
    power = jnp.zeros((hours, lanes), jnp.float32)
    more = lax.axis_index("hours") < lax.axis_size("hours") - 1
    copies = [pltpu.make_async_copy(new_ref.at[j], new_hbm.at[j], sems.at[j]) for j in range(count)]
    totals = []
    for j in range(count):
        rim = jnp.where(more, w_ref[EDGE * j : EDGE * (j + 1)], 0.0)
        later = lead_ref[j] + (jnp.concatenate([jnp.zeros((hours - EDGE, lanes), jnp.float32), rim], 0) + shifts[j])
        new = jnp.clip(base_ref[j] - (primal_step * scale_time) * later, 0.0, rows_ref[count + j : count + j + 1])
        new_ref[j] = new
        copies[j].start()
        extra = 2.0 * new - rel_ref[j]
        extra_ref[j] = extra
        power = power + (scale_sum * rows_ref[j : j + 1]) * extra
        totals.append(jnp.sum(extra, 0, keepdims=True))
    for j in range(count):
        tot[sinks[j]] = tot[sinks[j]] + totals[j]
    for i in range(2 * count):
        change = tot[i]
        if i < count:
            change = change + (stock_ref[i, hours - 1 : hours] - totals[i])
        tots_ref[i : i + 1] = change
    power_ref[...] = power
    windows(down_ref, delay_ref, extra_ref, stock_ref, mine_ref, theirs_ref, late_ref)
    for copy in copies:
        copy.wait()


def windows(down_ref, delay_ref, extra_ref, stock_ref, mine_ref, theirs_ref, late_ref):
    count, hours, lanes = extra_ref.shape
    lags = [delay_ref[j] for j in range(count)]
    sinks = [sink_of(down_ref, j, count) for j in range(count)]
    mine_ref[...] = jnp.zeros_like(mine_ref)
    theirs_ref[...] = jnp.zeros_like(theirs_ref)
    late_ref[...] = jnp.zeros_like(late_ref)
    place = lax.broadcasted_iota(jnp.int32, (RIM, lanes), 0)
    zeros = jnp.zeros((RIM, lanes), jnp.float32)
    for j in range(count):
        sums, total = scan_rows(extra_ref[j], False)
        arrived = place >= lags[j]
        tiles = [zeros] + turned([sums[k : k + RIM] for k in range(0, hours, RIM)], lags[j])
        window = jnp.concatenate([jnp.where(arrived, tiles[k + 1], tiles[k]) for k in range(hours // RIM)], 0)
        late_ref[sinks[j]] = late_ref[sinks[j]] + jnp.where(arrived, 0.0, tiles[-1] - total)

        @pl.when(sinks[j] < count)
        def _():
            at = pl.ds(pl.multiple_of(sinks[j] * hours, RIM), hours)
            mine_ref[at] = mine_ref[at] + window

        @pl.when((sinks[j] >= count) & (sinks[j] < 2 * count))
        def _():
            at = pl.ds(pl.multiple_of((sinks[j] - count) * hours, RIM), hours)
            theirs_ref[at] = theirs_ref[at] + window

        at = slice(j * hours, (j + 1) * hours)
        mine_ref[at] = mine_ref[at] + (stock_ref[j] - sums)
    for i in range(count):
        at = slice(count * hours + EDGE * i, count * hours + EDGE * (i + 1))
        mine_ref[at] = late_ref[i, 0:EDGE]
        theirs_ref[at] = late_ref[count + i, 0:EDGE]


def storage_kernel(scale_time, rows_ref, mine_ref, came_ref, rim_ref, off_ref, offcame_ref, sd_ref, power_ref, dual_ref, demand_ref, sd_hbm, excess_hbm, dual_out, sd_out, excess_out, sems):
    count, hours, lanes = sd_ref.shape
    earlier = lax.axis_index("hours") > 0
    copies = [[pltpu.make_async_copy(src.at[i], dst.at[i], sems.at[k, i]) for i in range(count)] for k, (src, dst) in enumerate(((sd_out, sd_hbm), (excess_out, excess_hbm)))]
    for i in range(count):
        row = [rows_ref[k * count + i : k * count + i + 1] for k in range(5)]
        at = slice(i * hours, (i + 1) * hours)
        change = mine_ref[at] + came_ref[at] + (off_ref[i : i + 1] + offcame_ref[i : i + 1])
        rim = jnp.concatenate([jnp.where(earlier, rim_ref[EDGE * i : EDGE * (i + 1)], 0.0), jnp.zeros((hours - EDGE, lanes), jnp.float32)], 0)
        storage = row[2] + scale_time * (change + rim)
        low, high = row[3], row[4]
        dual = sd_ref[i]
        sd_out[i] = dual + dual_step * storage - dual_step * jnp.clip(dual / dual_step + storage, low, high)
        copies[0][i].start()
        excess_out[i] = storage - jnp.clip(storage, low, high)
        copies[1][i].start()
    dual_out[...] = jnp.minimum(dual_ref[...] + dual_step * (power_ref[...] - demand_ref[...]), 0.0)
    for i in range(count):
        for k in range(2):
            copies[k][i].wait()


def passed_along(block, axis, distance):
    count = lax.axis_size(axis)
    return lax.ppermute(block, axis, [(i, (i + distance) % count) for i in range(count)])


def handed_on(block, axis, distance):
    devices = range(lax.axis_size(axis))
    return lax.ppermute(block, axis, [(i, i + distance) for i in devices if i + distance in devices])


def swapped(block, axis, bit):
    return lax.ppermute(block, axis, [(i, i ^ bit) for i in range(lax.axis_size(axis))])


def offsets(total, axis, reverse, beside):
    count, place = lax.axis_size(axis), lax.axis_index(axis)
    result = jnp.zeros_like(total)
    for step in range((count - 1).bit_length()):
        bit = 1 << step
        other = swapped(total, axis, bit)
        if step < len(beside) and beside[step]:
            other, *_ = lax.optimization_barrier((other, *beside[step]))
        low = (place & bit) == 0
        result = result + jnp.where(low if reverse else ~low, other, 0.0)
        total = total + other
    return result


def all_summed(part, axis):
    count, first = lax.axis_size(axis), None
    for step in range((count - 1).bit_length()):
        part = part + swapped(part, axis, 1 << step)
        first = part if first is None else first
    return part, first


SMEM = pl.BlockSpec(memory_space=pltpu.SMEM)
VMEM = pl.BlockSpec(memory_space=pltpu.VMEM)
HBM = pl.BlockSpec(memory_space=pltpu.HBM)


def call(body, ins, outs, scratch):
    return pl.pallas_call(
        body,
        out_shape=[jax.ShapeDtypeStruct(shape, jnp.float32) for _, shape in outs],
        in_specs=[spec for spec, _ in ins],
        out_specs=[spec for spec, _ in outs],
        scratch_shapes=[pltpu.VMEM(entry, jnp.float32) if isinstance(entry, tuple) else entry for entry in scratch],
        compiler_params=pltpu.CompilerParams(vmem_limit_bytes=32 * 1024 * 1024),
    )(*(array for _, array in ins))


def shards(
    release,
    storage_dual,
    demand_dual,
    cost,
    inflow,
    demand,
    storage_start,
    storage_low,
    storage_high,
    release_cap,
    efficiency,
    downstream,
    travel_delay,
):
    count, hours, lanes = release.shape
    scale_time = 1.0 / (hours * lax.axis_size("hours"))
    scale_sum = 1.0 / math.sqrt(count * lax.axis_size("river"))
    slab, flat, wide = (count, hours, lanes), (count, lanes), (count * (hours + EDGE), lanes)
    dma = pltpu.SemaphoreType.DMA

    (total,) = call(totals_kernel, [(VMEM, storage_dual)], [(VMEM, flat)], [])
    (sd_sent,) = call(copy_kernel, [(VMEM, lax.optimization_barrier((storage_dual, total))[0])], [(VMEM, slab)], [])
    sd_next = passed_along(sd_sent, "river", -1)
    base, rows = call(
        functools.partial(price_kernel, scale_sum),
        [(HBM, a) for a in (efficiency, release_cap, storage_start, storage_low, storage_high)] + [(VMEM, a) for a in (release, cost, demand_dual)],
        [(VMEM, slab), (VMEM, (5 * count, lanes))],
        [pltpu.SMEM((5, count), jnp.float32), dma((5,))],
    )
    (stock,) = call(stock_kernel, [(VMEM, inflow)], [(VMEM, slab)], [])
    lead, w = call(
        route_kernel,
        [(SMEM, downstream), (SMEM, travel_delay), (VMEM, storage_dual), (VMEM, sd_next)],
        [(VMEM, slab), (VMEM, (EDGE * count, lanes))],
        [(2 * count + 1, hours, lanes)],
    )
    off_own = offsets(total, "hours", True, [(base, rows), (lead, w), (stock,)])
    off_next = passed_along(off_own, "river", -1)
    w = passed_along(w, "hours", -1)
    release_new, mine, theirs, tots, power = call(
        functools.partial(release_kernel, scale_time, scale_sum),
        [(SMEM, downstream), (SMEM, travel_delay)] + [(VMEM, a) for a in (rows, base, lead, w, off_own, off_next, release, stock)],
        [(HBM, slab), (VMEM, wide), (VMEM, wide), (VMEM, (2 * count, lanes)), (VMEM, (hours, lanes))],
        [(2 * count + 1, 1, lanes), slab, slab, (2 * count + 1, RIM, lanes), dma((count,))],
    )
    supplied, first = all_summed(power, "river")
    came = passed_along(theirs, "river", 1)
    late = mine[count * hours :] + came[count * hours :]
    edge = handed_on(late, "hours", 1)
    off = offsets(tots, "hours", False, [(first,), (late, supplied)])
    off_came = passed_along(off[count:], "river", 1)
    storage_dual_new, storage_excess, demand_dual_new = call(
        functools.partial(storage_kernel, scale_time),
        [(VMEM, a) for a in (rows, mine, came, edge, off[:count], off_came, storage_dual, supplied, demand_dual, demand)],
        [(HBM, slab), (HBM, slab), (VMEM, (hours, lanes))],
        [slab, slab, dma((2, count))],
    )
    return (release_new, storage_dual_new, demand_dual_new, storage_excess)


def solution(mesh):
    field, flat, row = P("river", "hours", None), P("hours", None), P("river")
    return jax.shard_map(
        shards,
        mesh=mesh,
        in_specs=(field, field, flat, field, field, flat) + (row,) * 7,
        out_specs=(field, field, flat, field),
        check_vma=False,
    )
```

```python
import functools
import math

import jax
import jax.numpy as jnp
from jax import lax
from jax.experimental import pallas as pl
from jax.experimental.pallas import tpu as pltpu
from jax.sharding import PartitionSpec as P

DMAX = 6
RIM = 8
EDGE = DMAX - 1

primal_step = 1.0
dual_step = 0.1


def scan_rows(block, reverse):
    rows, lanes = block.shape
    place = lax.broadcasted_iota(jnp.int32, (8, lanes), 0)
    tiles = [block[k : k + 8] for k in range(0, rows, 8)]
    order = range(len(tiles) - 1, -1, -1) if reverse else range(len(tiles))
    carry = None
    for k in order:
        tile = tiles[k]
        for step in (1, 2, 4):
            moved = pltpu.roll(tile, 8 - step if reverse else step, 0)
            keep = place < 8 - step if reverse else place >= step
            tile = tile + jnp.where(keep, moved, 0.0)
        if carry is not None:
            tile = tile + carry
        tiles[k] = tile
        carry = tile[0:1] if reverse else tile[7:8]
    return jnp.concatenate(tiles, 0), carry


def sink_of(down_ref, j, count):
    down = down_ref[j]
    base = lax.axis_index("river") * count
    return jnp.where(down < 0, 2 * count, down - base)


def turned(tiles, amount):
    return [pltpu.roll(tile, amount, 0) for tile in tiles]


def totals_kernel(sd_ref, total_ref):
    for i in range(sd_ref.shape[0]):
        total_ref[i : i + 1] = jnp.sum(sd_ref[i], 0, keepdims=True)


def price_kernel(scale_sum, eff_hbm, cap_hbm, start_hbm, low_hbm, high_hbm, rel_ref, cost_ref, dual_ref, base_ref, rows_ref, scalars, sems):
    count, hours, lanes = base_ref.shape
    small = (eff_hbm, cap_hbm, start_hbm, low_hbm, high_hbm)
    copies = [pltpu.make_async_copy(ref, scalars.at[k], sems.at[k]) for k, ref in enumerate(small)]
    for copy in copies:
        copy.start()
    for copy in copies:
        copy.wait()
    dual = dual_ref[...]
    for j in range(count):
        for k in range(5):
            at = k * count + j
            rows_ref[at : at + 1] = jnp.full((1, lanes), scalars[k, j], jnp.float32)
        base_ref[j] = rel_ref[j] - primal_step * (cost_ref[j] + (scale_sum * scalars[0, j]) * dual)


def stock_kernel(inflow_ref, stock_ref):
    for j in range(inflow_ref.shape[0]):
        stock_ref[j] = scan_rows(inflow_ref[j], False)[0]


def copy_kernel(in_ref, out_ref):
    out_ref[...] = in_ref[...]


def route_kernel(down_ref, delay_ref, sd_ref, next_ref, lead_ref, w_ref, sums_ref):
    count, hours, lanes = sd_ref.shape
    for i in range(2 * count):
        ref, k = (sd_ref, i) if i < count else (next_ref, i - count)
        sums_ref[i] = scan_rows(ref[k], True)[0]
    sums_ref[2 * count] = jnp.zeros((hours, lanes), jnp.float32)
    place = lax.broadcasted_iota(jnp.int32, (RIM, lanes), 0)
    for j in range(count):
        lag = delay_ref[j]
        sink = sums_ref[sink_of(down_ref, j, count)]
        inside = place < RIM - lag
        tiles = turned([sink[k : k + RIM] for k in range(0, hours, RIM)], RIM - lag)
        w_ref[EDGE * j : EDGE * (j + 1)] = jnp.where(inside, 0.0, tiles[0] - sink[0:1])[RIM - EDGE :]
        tiles.append(jnp.zeros((RIM, lanes), jnp.float32))
        later = jnp.concatenate([jnp.where(inside, tiles[k], tiles[k + 1]) for k in range(hours // RIM)], 0)
        lead_ref[j] = later - sums_ref[j]


def release_kernel(scale_time, scale_sum, down_ref, delay_ref, rows_ref, base_ref, lead_ref, w_ref, own_ref, next_ref, rel_ref, stock_ref, new_ref, extra_ref, minerim_ref, theirsrim_ref, tots_ref, power_ref, tot, late_ref):
    count, hours, lanes = base_ref.shape
    for i in range(count):
        tot[i] = own_ref[i : i + 1]
        tot[count + i] = next_ref[i : i + 1]
    tot[2 * count] = jnp.zeros((1, lanes), jnp.float32)
    sinks = [sink_of(down_ref, j, count) for j in range(count)]
    shifts = [tot[sinks[j]] - tot[j] for j in range(count)]
    tot[...] = jnp.zeros_like(tot)
    power = jnp.zeros((hours, lanes), jnp.float32)
    more = lax.axis_index("hours") < lax.axis_size("hours") - 1
    totals = []
    for j in range(count):
        rim = jnp.where(more, w_ref[EDGE * j : EDGE * (j + 1)], 0.0)
        later = lead_ref[j] + (jnp.concatenate([jnp.zeros((hours - EDGE, lanes), jnp.float32), rim], 0) + shifts[j])
        new = jnp.clip(base_ref[j] - (primal_step * scale_time) * later, 0.0, rows_ref[count + j : count + j + 1])
        new_ref[j] = new
        extra = 2.0 * new - rel_ref[j]
        extra_ref[j] = extra
        power = power + (scale_sum * rows_ref[j : j + 1]) * extra
        totals.append(jnp.sum(extra, 0, keepdims=True))
    for j in range(count):
        tot[sinks[j]] = tot[sinks[j]] + totals[j]
    late_ref[...] = jnp.zeros_like(late_ref)
    place = lax.broadcasted_iota(jnp.int32, (RIM, lanes), 0)
    for j in range(count):
        lag = delay_ref[j]
        last = extra_ref[j, hours - RIM :]
        after = pltpu.roll(scan_rows(last, True)[0] - last, lag, 0)
        late_ref[sinks[j]] = late_ref[sinks[j]] - jnp.where(place < lag, after, 0.0)
    for i in range(count):
        at = slice(EDGE * i, EDGE * (i + 1))
        minerim_ref[at] = late_ref[i, 0:EDGE]
        theirsrim_ref[at] = late_ref[count + i, 0:EDGE]
    for i in range(2 * count):
        change = tot[i]
        if i < count:
            change = change + (stock_ref[i, hours - 1 : hours] - totals[i])
        tots_ref[i : i + 1] = change
    power_ref[...] = power


def windows_kernel(down_ref, delay_ref, extra_ref, stock_ref, new_ref, new_hbm, mine_ref, theirs_ref, sem):
    copy = pltpu.make_async_copy(new_ref, new_hbm, sem)
    copy.start()
    count, hours, lanes = extra_ref.shape
    lags = [delay_ref[j] for j in range(count)]
    sinks = [sink_of(down_ref, j, count) for j in range(count)]
    mine_ref[...] = jnp.zeros_like(mine_ref)
    theirs_ref[...] = jnp.zeros_like(theirs_ref)
    place = lax.broadcasted_iota(jnp.int32, (RIM, lanes), 0)
    zeros = jnp.zeros((RIM, lanes), jnp.float32)
    for j in range(count):
        sums, _ = scan_rows(extra_ref[j], False)
        arrived = place >= lags[j]
        tiles = [zeros] + turned([sums[k : k + RIM] for k in range(0, hours, RIM)], lags[j])
        window = jnp.concatenate([jnp.where(arrived, tiles[k + 1], tiles[k]) for k in range(hours // RIM)], 0)

        @pl.when(sinks[j] < count)
        def _():
            at = pl.ds(pl.multiple_of(sinks[j] * hours, RIM), hours)
            mine_ref[at] = mine_ref[at] + window

        @pl.when((sinks[j] >= count) & (sinks[j] < 2 * count))
        def _():
            at = pl.ds(pl.multiple_of((sinks[j] - count) * hours, RIM), hours)
            theirs_ref[at] = theirs_ref[at] + window

        at = slice(j * hours, (j + 1) * hours)
        mine_ref[at] = mine_ref[at] + (stock_ref[j] - sums)
    copy.wait()


def storage_kernel(scale_time, rows_ref, mine_ref, came_ref, rim_ref, off_ref, sd_ref, power_ref, dual_ref, demand_ref, sd_hbm, excess_hbm, dual_hbm, sd_out, excess_out, dual_out, sems, dual_sem):
    count, hours, lanes = sd_ref.shape
    earlier = lax.axis_index("hours") > 0
    copies = [[pltpu.make_async_copy(src.at[i], dst.at[i], sems.at[k, i]) for i in range(count)] for k, (src, dst) in enumerate(((sd_out, sd_hbm), (excess_out, excess_hbm)))]
    dual_out[...] = jnp.minimum(dual_ref[...] + dual_step * (power_ref[...] - demand_ref[...]), 0.0)
    dual_copy = pltpu.make_async_copy(dual_out, dual_hbm, dual_sem)
    dual_copy.start()
    for i in range(count):
        row = [rows_ref[k * count + i : k * count + i + 1] for k in range(5)]
        level, low, high = row[2] + scale_time * off_ref[i : i + 1], row[3], row[4]
        low_dual, high_dual = dual_step * low, dual_step * high
        for k in range(0, hours, RIM):
            at = slice(i * hours + k, i * hours + k + RIM)
            change = mine_ref[at] + came_ref[at]
            if k == 0:
                rim = jnp.where(earlier, rim_ref[EDGE * i : EDGE * (i + 1)], 0.0)
                change = change + jnp.concatenate([rim, jnp.zeros((RIM - EDGE, lanes), jnp.float32)], 0)
            storage = level + scale_time * change
            ahead = sd_ref[i, k : k + RIM] + dual_step * storage
            sd_out[i, k : k + RIM] = ahead - jnp.clip(ahead, low_dual, high_dual)
            excess_out[i, k : k + RIM] = storage - jnp.clip(storage, low, high)
        copies[0][i].start()
        copies[1][i].start()
    for i in range(count):
        for k in range(2):
            copies[k][i].wait()
    dual_copy.wait()


def passed_along(block, axis, distance):
    count = lax.axis_size(axis)
    return lax.ppermute(block, axis, [(i, (i + distance) % count) for i in range(count)])


def swapped(block, axis, bit):
    return lax.ppermute(block, axis, [(i, i ^ bit) for i in range(lax.axis_size(axis))])


def all_summed(part, axis, done):
    for step in range(done, (lax.axis_size(axis) - 1).bit_length()):
        part = part + swapped(part, axis, 1 << step)
    return part


def offsets(total, axis, reverse, beside):
    count, place = lax.axis_size(axis), lax.axis_index(axis)
    result = jnp.zeros_like(total)
    for step in range((count - 1).bit_length()):
        bit = 1 << step
        other = swapped(total, axis, bit)
        if step < len(beside) and beside[step]:
            other, *_ = lax.optimization_barrier((other, *beside[step]))
        low = (place & bit) == 0
        result = result + jnp.where(low if reverse else ~low, other, 0.0)
        total = total + other
    return result


SMEM = pl.BlockSpec(memory_space=pltpu.SMEM)
VMEM = pl.BlockSpec(memory_space=pltpu.VMEM)
HBM = pl.BlockSpec(memory_space=pltpu.HBM)


def call(body, ins, outs, scratch):
    return pl.pallas_call(
        body,
        out_shape=[jax.ShapeDtypeStruct(shape, jnp.float32) for _, shape in outs],
        in_specs=[spec for spec, _ in ins],
        out_specs=[spec for spec, _ in outs],
        scratch_shapes=[pltpu.VMEM(entry, jnp.float32) if isinstance(entry, tuple) else entry for entry in scratch],
        compiler_params=pltpu.CompilerParams(vmem_limit_bytes=32 * 1024 * 1024),
    )(*(array for _, array in ins))


def shards(
    release,
    storage_dual,
    demand_dual,
    cost,
    inflow,
    demand,
    storage_start,
    storage_low,
    storage_high,
    release_cap,
    efficiency,
    downstream,
    travel_delay,
):
    count, hours, lanes = release.shape
    scale_time = 1.0 / (hours * lax.axis_size("hours"))
    scale_sum = 1.0 / math.sqrt(count * lax.axis_size("river"))
    slab, flat = (count, hours, lanes), (count, lanes)
    wide, edges = (count * hours, lanes), (count * EDGE, lanes)
    dma = pltpu.SemaphoreType.DMA

    (total,) = call(totals_kernel, [(VMEM, storage_dual)], [(VMEM, flat)], [])
    (sd_sent,) = call(copy_kernel, [(VMEM, lax.optimization_barrier((storage_dual, total))[0])], [(VMEM, slab)], [])
    sd_next = passed_along(sd_sent, "river", -1)
    base, rows = call(
        functools.partial(price_kernel, scale_sum),
        [(HBM, a) for a in (efficiency, release_cap, storage_start, storage_low, storage_high)] + [(VMEM, a) for a in (release, cost, demand_dual)],
        [(VMEM, slab), (VMEM, (5 * count, lanes))],
        [pltpu.SMEM((5, count), jnp.float32), dma((5,))],
    )
    (stock,) = call(stock_kernel, [(VMEM, inflow)], [(VMEM, slab)], [])
    lead, w_sent = call(
        route_kernel,
        [(SMEM, downstream), (SMEM, travel_delay), (VMEM, storage_dual), (VMEM, sd_next)],
        [(VMEM, slab), (VMEM, edges)],
        [(2 * count + 1, hours, lanes)],
    )
    w = passed_along(w_sent, "hours", -1)
    off_own = offsets(total, "hours", True, [(base, rows), (lead, w_sent), (stock,)])
    off_next = passed_along(off_own, "river", -1)

    new, extra, rim_mine, rim_theirs, tots, power = call(
        functools.partial(release_kernel, scale_time, scale_sum),
        [(SMEM, downstream), (SMEM, travel_delay)] + [(VMEM, a) for a in (rows, base, lead, w, off_own, off_next, release, stock)],
        [(VMEM, slab), (VMEM, slab), (VMEM, edges), (VMEM, edges), (VMEM, (2 * count, lanes)), (VMEM, (hours, lanes))],
        [(2 * count + 1, 1, lanes), (2 * count + 1, RIM, lanes)],
    )
    release_new, mine, theirs = call(
        windows_kernel,
        [(SMEM, downstream), (SMEM, travel_delay)] + [(VMEM, a) for a in (extra, stock, new)],
        [(HBM, slab), (VMEM, wide), (VMEM, wide)],
        [dma],
    )

    power = power + swapped(power, "river", 1)
    pairs = lax.axis_size("river") == 4
    if pairs:
        moved = passed_along(jnp.concatenate([rim_theirs, power], 0), "river", 1)
        late = rim_mine + moved[: count * EDGE]
        whole = power + moved[count * EDGE :]
    else:
        late = rim_mine + passed_along(rim_theirs, "river", 1)
    tot_came = passed_along(tots[count:], "river", 1)
    tot_came, theirs, mine, power = lax.optimization_barrier((tot_came, theirs, mine, power))
    came = passed_along(theirs, "river", 1)
    edge = passed_along(late, "hours", 1)
    place, steps = lax.axis_index("hours"), (lax.axis_size("hours") - 1).bit_length()
    tot = tots[:count] + tot_came
    off = jnp.zeros_like(tot)
    for step in range(steps):
        other = swapped(tot, "hours", 1 << step)
        if step == 0:
            other, late = lax.optimization_barrier((other, late))
            if pairs:
                supplied = jnp.where(lax.axis_index("river") % 2 == 0, whole, swapped(whole, "river", 1))
            else:
                supplied = all_summed(power, "river", 1)
        if step == 1:
            other, came = lax.optimization_barrier((other, came))
        if step == steps - 1:
            other, edge = lax.optimization_barrier((other, edge))
        off = off + jnp.where((place & (1 << step)) != 0, other, 0.0)
        tot = tot + other
    storage_dual_new, storage_excess, demand_dual_new = call(
        functools.partial(storage_kernel, scale_time),
        [(VMEM, a) for a in (rows, mine, came, edge, off, storage_dual, supplied, demand_dual, demand)],
        [(HBM, slab), (HBM, slab), (HBM, (hours, lanes))],
        [slab, slab, (hours, lanes), dma((2, count)), dma],
    )
    return (release_new, storage_dual_new, demand_dual_new, storage_excess)


def solution(mesh):
    field, flat, row = P("river", "hours", None), P("hours", None), P("river")
    return jax.shard_map(
        shards,
        mesh=mesh,
        in_specs=(field, field, flat, field, field, flat) + (row,) * 7,
        out_specs=(field, field, flat, field),
        check_vma=False,
    )
```

```python
import functools
import math

import jax
import jax.numpy as jnp
from jax import lax
from jax.experimental import pallas as pl
from jax.experimental.pallas import tpu as pltpu
from jax.sharding import PartitionSpec as P

DMAX = 6
RIM = 8
EDGE = DMAX - 1

primal_step = 1.0
dual_step = 0.1


def scan_rows(block, reverse):
    rows, lanes = block.shape
    place = lax.broadcasted_iota(jnp.int32, (8, lanes), 0)
    tiles = [block[k : k + 8] for k in range(0, rows, 8)]
    order = range(len(tiles) - 1, -1, -1) if reverse else range(len(tiles))
    carry = None
    for k in order:
        tile = tiles[k]
        for step in (1, 2, 4):
            moved = pltpu.roll(tile, 8 - step if reverse else step, 0)
            keep = place < 8 - step if reverse else place >= step
            tile = tile + jnp.where(keep, moved, 0.0)
        if carry is not None:
            tile = tile + carry
        tiles[k] = tile
        carry = tile[0:1] if reverse else tile[7:8]
    return jnp.concatenate(tiles, 0), carry


def routes(down_ref, delay_ref):
    down, delay = down_ref[...], delay_ref[...]
    (count,) = down.shape
    base = lax.axis_index("river") * count
    return [jnp.where(down[j] < 0, 2 * count, down[j] - base) for j in range(count)], [delay[j] for j in range(count)]


def turned(tiles, amount):
    return [pltpu.roll(tile, amount, 0) for tile in tiles]


def totals_kernel(sd_ref, total_ref):
    for i in range(sd_ref.shape[0]):
        total_ref[i : i + 1] = jnp.sum(sd_ref[i], 0, keepdims=True)


def price_kernel(scale_sum, eff_ref, cap_ref, start_ref, low_ref, high_ref, rel_ref, cost_ref, dual_ref, base_ref, rows_ref):
    count, hours, lanes = base_ref.shape
    dual = dual_ref[...]
    scalars = [ref[...] for ref in (eff_ref, cap_ref, start_ref, low_ref, high_ref)]
    for j in range(count):
        for k in range(5):
            at = k * count + j
            rows_ref[at : at + 1] = jnp.full((1, lanes), scalars[k][j], jnp.float32)
        base_ref[j] = rel_ref[j] - primal_step * (cost_ref[j] + (scale_sum * scalars[0][j]) * dual)


def stock_kernel(inflow_ref, stock_ref):
    for j in range(inflow_ref.shape[0]):
        stock_ref[j] = scan_rows(inflow_ref[j], False)[0]


def copy_kernel(in_ref, out_ref):
    out_ref[...] = in_ref[...]


def route_kernel(down_ref, delay_ref, sd_ref, next_ref, lead_ref, w_ref, sums_ref):
    count, hours, lanes = sd_ref.shape
    for i in range(2 * count):
        ref, k = (sd_ref, i) if i < count else (next_ref, i - count)
        sums_ref[i] = scan_rows(ref[k], True)[0]
    sums_ref[2 * count] = jnp.zeros((hours, lanes), jnp.float32)
    place = lax.broadcasted_iota(jnp.int32, (RIM, lanes), 0)
    sinks, lags = routes(down_ref, delay_ref)
    for j in range(count):
        lag = lags[j]
        sink = sums_ref[sinks[j]]
        inside = place < RIM - lag
        tiles = turned([sink[k : k + RIM] for k in range(0, hours, RIM)], RIM - lag)
        w_ref[EDGE * j : EDGE * (j + 1)] = jnp.where(inside, 0.0, tiles[0] - sink[0:1])[RIM - EDGE :]
        tiles.append(jnp.zeros((RIM, lanes), jnp.float32))
        later = jnp.concatenate([jnp.where(inside, tiles[k], tiles[k + 1]) for k in range(hours // RIM)], 0)
        lead_ref[j] = later - sums_ref[j]


def release_kernel(scale_time, scale_sum, down_ref, delay_ref, rows_ref, base_ref, lead_ref, w_ref, own_ref, next_ref, rel_ref, stock_ref, new_ref, extra_ref, minerim_ref, theirsrim_ref, tots_ref, power_ref, tot, late_ref):
    count, hours, lanes = base_ref.shape
    for i in range(count):
        tot[i] = own_ref[i : i + 1]
        tot[count + i] = next_ref[i : i + 1]
    tot[2 * count] = jnp.zeros((1, lanes), jnp.float32)
    sinks, lags = routes(down_ref, delay_ref)
    shifts = [tot[sinks[j]] - tot[j] for j in range(count)]
    tot[...] = jnp.zeros_like(tot)
    power = jnp.zeros((hours, lanes), jnp.float32)
    more = lax.axis_index("hours") < lax.axis_size("hours") - 1
    totals = []
    for j in range(count):
        rim = jnp.where(more, w_ref[EDGE * j : EDGE * (j + 1)], 0.0)
        later = lead_ref[j] + (jnp.concatenate([jnp.zeros((hours - EDGE, lanes), jnp.float32), rim], 0) + shifts[j])
        new = jnp.clip(base_ref[j] - (primal_step * scale_time) * later, 0.0, rows_ref[count + j : count + j + 1])
        new_ref[j] = new
        extra = 2.0 * new - rel_ref[j]
        extra_ref[j] = extra
        power = power + (scale_sum * rows_ref[j : j + 1]) * extra
        totals.append(jnp.sum(extra, 0, keepdims=True))
    for j in range(count):
        tot[sinks[j]] = tot[sinks[j]] + totals[j]
    late_ref[...] = jnp.zeros_like(late_ref)
    place = lax.broadcasted_iota(jnp.int32, (RIM, lanes), 0)
    for j in range(count):
        lag = lags[j]
        last = extra_ref[j, hours - RIM :]
        after = pltpu.roll(scan_rows(last, True)[0] - last, lag, 0)
        late_ref[sinks[j]] = late_ref[sinks[j]] - jnp.where(place < lag, after, 0.0)
    for i in range(count):
        at = slice(EDGE * i, EDGE * (i + 1))
        minerim_ref[at] = late_ref[i, 0:EDGE]
        theirsrim_ref[at] = late_ref[count + i, 0:EDGE]
    for i in range(2 * count):
        change = tot[i]
        if i < count:
            change = change + (stock_ref[i, hours - 1 : hours] - totals[i])
        tots_ref[i : i + 1] = change
    power_ref[...] = power


def windows_kernel(down_ref, delay_ref, extra_ref, stock_ref, new_ref, new_hbm, mine_ref, theirs_ref, sem):
    copy = pltpu.make_async_copy(new_ref, new_hbm, sem)
    copy.start()
    count, hours, lanes = extra_ref.shape
    sinks, lags = routes(down_ref, delay_ref)
    mine_ref[...] = jnp.zeros_like(mine_ref)
    theirs_ref[...] = jnp.zeros_like(theirs_ref)
    place = lax.broadcasted_iota(jnp.int32, (RIM, lanes), 0)
    zeros = jnp.zeros((RIM, lanes), jnp.float32)
    for j in range(count):
        sums, _ = scan_rows(extra_ref[j], False)
        arrived = place >= lags[j]
        tiles = [zeros] + turned([sums[k : k + RIM] for k in range(0, hours, RIM)], lags[j])
        window = jnp.concatenate([jnp.where(arrived, tiles[k + 1], tiles[k]) for k in range(hours // RIM)], 0)

        @pl.when(sinks[j] < count)
        def _():
            at = pl.ds(pl.multiple_of(sinks[j] * hours, RIM), hours)
            mine_ref[at] = mine_ref[at] + window

        @pl.when((sinks[j] >= count) & (sinks[j] < 2 * count))
        def _():
            at = pl.ds(pl.multiple_of((sinks[j] - count) * hours, RIM), hours)
            theirs_ref[at] = theirs_ref[at] + window

        at = slice(j * hours, (j + 1) * hours)
        mine_ref[at] = mine_ref[at] + (stock_ref[j] - sums)
    copy.wait()


def storage_kernel(scale_time, rows_ref, mine_ref, came_ref, rim_ref, off_ref, sd_ref, power_ref, dual_ref, demand_ref, sd_hbm, excess_hbm, dual_hbm, sd_out, excess_out, dual_out, sems, dual_sem):
    count, hours, lanes = sd_ref.shape
    earlier = lax.axis_index("hours") > 0
    copies = [[pltpu.make_async_copy(src.at[i], dst.at[i], sems.at[k, i]) for i in range(count)] for k, (src, dst) in enumerate(((sd_out, sd_hbm), (excess_out, excess_hbm)))]
    dual_out[...] = jnp.minimum(dual_ref[...] + dual_step * (power_ref[...] - demand_ref[...]), 0.0)
    dual_copy = pltpu.make_async_copy(dual_out, dual_hbm, dual_sem)
    dual_copy.start()
    for i in range(count):
        row = [rows_ref[k * count + i : k * count + i + 1] for k in range(5)]
        level, low, high = row[2] + scale_time * off_ref[i : i + 1], row[3], row[4]
        low_dual, high_dual = dual_step * low, dual_step * high
        for k in range(0, hours, RIM):
            at = slice(i * hours + k, i * hours + k + RIM)
            change = mine_ref[at] + came_ref[at]
            if k == 0:
                rim = jnp.where(earlier, rim_ref[EDGE * i : EDGE * (i + 1)], 0.0)
                change = change + jnp.concatenate([rim, jnp.zeros((RIM - EDGE, lanes), jnp.float32)], 0)
            storage = level + scale_time * change
            ahead = sd_ref[i, k : k + RIM] + dual_step * storage
            sd_out[i, k : k + RIM] = ahead - jnp.clip(ahead, low_dual, high_dual)
            excess_out[i, k : k + RIM] = storage - jnp.clip(storage, low, high)
        copies[0][i].start()
        copies[1][i].start()
    for i in range(count):
        for k in range(2):
            copies[k][i].wait()
    dual_copy.wait()


def passed_along(block, axis, distance):
    count = lax.axis_size(axis)
    return lax.ppermute(block, axis, [(i, (i + distance) % count) for i in range(count)])


def swapped(block, axis, bit):
    return lax.ppermute(block, axis, [(i, i ^ bit) for i in range(lax.axis_size(axis))])


def all_summed(part, axis, done):
    for step in range(done, (lax.axis_size(axis) - 1).bit_length()):
        part = part + swapped(part, axis, 1 << step)
    return part


def offsets(total, axis, reverse, beside):
    count, place = lax.axis_size(axis), lax.axis_index(axis)
    result = jnp.zeros_like(total)
    for step in range((count - 1).bit_length()):
        bit = 1 << step
        other = swapped(total, axis, bit)
        if step < len(beside) and beside[step]:
            other, *_ = lax.optimization_barrier((other, *beside[step]))
        low = (place & bit) == 0
        result = result + jnp.where(low if reverse else ~low, other, 0.0)
        total = total + other
    return result


VMEM = pl.BlockSpec(memory_space=pltpu.VMEM)
HBM = pl.BlockSpec(memory_space=pltpu.HBM)


def call(body, ins, outs, scratch):
    return pl.pallas_call(
        body,
        out_shape=[jax.ShapeDtypeStruct(shape, jnp.float32) for _, shape in outs],
        in_specs=[spec for spec, _ in ins],
        out_specs=[spec for spec, _ in outs],
        scratch_shapes=[pltpu.VMEM(entry, jnp.float32) if isinstance(entry, tuple) else entry for entry in scratch],
        compiler_params=pltpu.CompilerParams(vmem_limit_bytes=32 * 1024 * 1024),
    )(*(array for _, array in ins))


def shards(
    release,
    storage_dual,
    demand_dual,
    cost,
    inflow,
    demand,
    storage_start,
    storage_low,
    storage_high,
    release_cap,
    efficiency,
    downstream,
    travel_delay,
):
    count, hours, lanes = release.shape
    scale_time = 1.0 / (hours * lax.axis_size("hours"))
    scale_sum = 1.0 / math.sqrt(count * lax.axis_size("river"))
    slab, flat = (count, hours, lanes), (count, lanes)
    wide, edges = (count * hours, lanes), (count * EDGE, lanes)
    dma = pltpu.SemaphoreType.DMA

    (total,) = call(totals_kernel, [(VMEM, storage_dual)], [(VMEM, flat)], [])
    (sd_sent,) = call(copy_kernel, [(VMEM, lax.optimization_barrier((storage_dual, total))[0])], [(VMEM, slab)], [])
    sd_next = passed_along(sd_sent, "river", -1)
    base, rows = call(
        functools.partial(price_kernel, scale_sum),
        [(VMEM, a) for a in (efficiency, release_cap, storage_start, storage_low, storage_high, release, cost, demand_dual)],
        [(VMEM, slab), (VMEM, (5 * count, lanes))],
        [],
    )
    (stock,) = call(stock_kernel, [(VMEM, inflow)], [(VMEM, slab)], [])
    lead, w_sent = call(
        route_kernel,
        [(VMEM, a) for a in (downstream, travel_delay, storage_dual, sd_next)],
        [(VMEM, slab), (VMEM, edges)],
        [(2 * count + 1, hours, lanes)],
    )
    w = passed_along(w_sent, "hours", -1)
    off_own = offsets(total, "hours", True, [(base, rows), (lead, w_sent), (stock,)])
    off_next = passed_along(off_own, "river", -1)

    new, extra, rim_mine, rim_theirs, tots, power = call(
        functools.partial(release_kernel, scale_time, scale_sum),
        [(VMEM, a) for a in (downstream, travel_delay, rows, base, lead, w, off_own, off_next, release, stock)],
        [(VMEM, slab), (VMEM, slab), (VMEM, edges), (VMEM, edges), (VMEM, (2 * count, lanes)), (VMEM, (hours, lanes))],
        [(2 * count + 1, 1, lanes), (2 * count + 1, RIM, lanes)],
    )
    release_new, mine, theirs = call(
        windows_kernel,
        [(VMEM, a) for a in (downstream, travel_delay, extra, stock, new)],
        [(HBM, slab), (VMEM, wide), (VMEM, wide)],
        [dma],
    )

    tot_came = passed_along(tots[count:], "river", 1)
    power = power + swapped(power, "river", 1)
    pairs = lax.axis_size("river") == 4
    if pairs:
        moved = passed_along(jnp.concatenate([rim_theirs, power], 0), "river", 1)
        late = rim_mine + moved[: count * EDGE]
        whole = power + moved[count * EDGE :]
    else:
        late = rim_mine + passed_along(rim_theirs, "river", 1)
    tot_came, theirs, mine, power = lax.optimization_barrier((tot_came, theirs, mine, power))
    came = passed_along(theirs, "river", 1)
    edge = passed_along(late, "hours", 1)
    place, steps = lax.axis_index("hours"), (lax.axis_size("hours") - 1).bit_length()
    tot = tots[:count] + tot_came
    off = jnp.zeros_like(tot)
    for step in range(steps):
        other = swapped(tot, "hours", 1 << step)
        if step == 0:
            other, late = lax.optimization_barrier((other, late))
            if pairs:
                supplied = jnp.where(lax.axis_index("river") % 2 == 0, whole, swapped(whole, "river", 1))
            else:
                supplied = all_summed(power, "river", 1)
        if step == 1:
            other, came = lax.optimization_barrier((other, came))
        if step == steps - 1:
            other, edge = lax.optimization_barrier((other, edge))
        off = off + jnp.where((place & (1 << step)) != 0, other, 0.0)
        tot = tot + other
    storage_dual_new, storage_excess, demand_dual_new = call(
        functools.partial(storage_kernel, scale_time),
        [(VMEM, a) for a in (rows, mine, came, edge, off, storage_dual, supplied, demand_dual, demand)],
        [(HBM, slab), (HBM, slab), (HBM, (hours, lanes))],
        [slab, slab, (hours, lanes), dma((2, count)), dma],
    )
    return (release_new, storage_dual_new, demand_dual_new, storage_excess)


def solution(mesh):
    field, flat, row = P("river", "hours", None), P("hours", None), P("river")
    return jax.shard_map(
        shards,
        mesh=mesh,
        in_specs=(field, field, flat, field, field, flat) + (row,) * 7,
        out_specs=(field, field, flat, field),
        check_vma=False,
    )
```

```python
import functools
import math

import jax
import jax.numpy as jnp
from jax import lax
from jax.experimental import pallas as pl
from jax.experimental.pallas import tpu as pltpu
from jax.sharding import PartitionSpec as P

DMAX = 6
RIM = 8
EDGE = DMAX - 1

primal_step = 1.0
dual_step = 0.1


def scan_rows(block, reverse):
    rows, lanes = block.shape
    place = lax.broadcasted_iota(jnp.int32, (8, lanes), 0)
    tiles = [block[k : k + 8] for k in range(0, rows, 8)]
    order = range(len(tiles) - 1, -1, -1) if reverse else range(len(tiles))
    carry = None
    for k in order:
        tile = tiles[k]
        for step in (1, 2, 4):
            moved = pltpu.roll(tile, 8 - step if reverse else step, 0)
            keep = place < 8 - step if reverse else place >= step
            tile = tile + jnp.where(keep, moved, 0.0)
        if carry is not None:
            tile = tile + carry
        tiles[k] = tile
        carry = tile[0:1] if reverse else tile[7:8]
    return jnp.concatenate(tiles, 0), carry


def routes(down_ref, delay_ref):
    down, delay = down_ref[...], delay_ref[...]
    (count,) = down.shape
    base = lax.axis_index("river") * count
    return [jnp.where(down[j] < 0, 2 * count, down[j] - base) for j in range(count)], [delay[j] for j in range(count)]


def turned(tiles, amount):
    return [pltpu.roll(tile, amount, 0) for tile in tiles]


def totals_kernel(sd_ref, total_ref):
    for i in range(sd_ref.shape[0]):
        total_ref[i : i + 1] = jnp.sum(sd_ref[i], 0, keepdims=True)


def price_kernel(scale_sum, eff_ref, cap_ref, start_ref, low_ref, high_ref, rel_ref, cost_ref, dual_ref, base_ref, rows_ref):
    count, hours, lanes = base_ref.shape
    dual = dual_ref[...]
    scalars = [ref[...] for ref in (eff_ref, cap_ref, start_ref, low_ref, high_ref)]
    for j in range(count):
        for k in range(5):
            at = k * count + j
            rows_ref[at : at + 1] = jnp.full((1, lanes), scalars[k][j], jnp.float32)
        base_ref[j] = rel_ref[j] - primal_step * (cost_ref[j] + (scale_sum * scalars[0][j]) * dual)


def stock_kernel(inflow_ref, stock_ref):
    for j in range(inflow_ref.shape[0]):
        stock_ref[j] = scan_rows(inflow_ref[j], False)[0]


def copy_kernel(in_ref, out_ref):
    out_ref[...] = in_ref[...]


def route_kernel(down_ref, delay_ref, sd_ref, next_ref, lead_ref, w_ref, sums_ref):
    count, hours, lanes = sd_ref.shape
    for i in range(2 * count):
        ref, k = (sd_ref, i) if i < count else (next_ref, i - count)
        sums_ref[i] = scan_rows(ref[k], True)[0]
    sums_ref[2 * count] = jnp.zeros((hours, lanes), jnp.float32)
    place = lax.broadcasted_iota(jnp.int32, (RIM, lanes), 0)
    sinks, lags = routes(down_ref, delay_ref)
    for j in range(count):
        lag = lags[j]
        sink = sums_ref[sinks[j]]
        inside = place < RIM - lag
        tiles = turned([sink[k : k + RIM] for k in range(0, hours, RIM)], RIM - lag)
        w_ref[EDGE * j : EDGE * (j + 1)] = jnp.where(inside, 0.0, tiles[0] - sink[0:1])[RIM - EDGE :]
        tiles.append(jnp.zeros((RIM, lanes), jnp.float32))
        later = jnp.concatenate([jnp.where(inside, tiles[k], tiles[k + 1]) for k in range(hours // RIM)], 0)
        lead_ref[j] = later - sums_ref[j]


def release_kernel(scale_time, scale_sum, down_ref, delay_ref, rows_ref, base_ref, lead_ref, w_ref, own_ref, next_ref, rel_ref, stock_ref, new_ref, extra_ref, minerim_ref, theirsrim_ref, tots_ref, power_ref, tot, late_ref):
    count, hours, lanes = base_ref.shape
    for i in range(count):
        tot[i] = own_ref[i : i + 1]
        tot[count + i] = next_ref[i : i + 1]
    tot[2 * count] = jnp.zeros((1, lanes), jnp.float32)
    sinks, lags = routes(down_ref, delay_ref)
    shifts = [tot[sinks[j]] - tot[j] for j in range(count)]
    tot[...] = jnp.zeros_like(tot)
    power = jnp.zeros((hours, lanes), jnp.float32)
    more = lax.axis_index("hours") < lax.axis_size("hours") - 1
    totals = []
    for j in range(count):
        rim = jnp.where(more, w_ref[EDGE * j : EDGE * (j + 1)], 0.0)
        later = lead_ref[j] + (jnp.concatenate([jnp.zeros((hours - EDGE, lanes), jnp.float32), rim], 0) + shifts[j])
        new = jnp.clip(base_ref[j] - (primal_step * scale_time) * later, 0.0, rows_ref[count + j : count + j + 1])
        new_ref[j] = new
        extra = 2.0 * new - rel_ref[j]
        extra_ref[j] = extra
        power = power + (scale_sum * rows_ref[j : j + 1]) * extra
        totals.append(jnp.sum(extra, 0, keepdims=True))
    for j in range(count):
        tot[sinks[j]] = tot[sinks[j]] + totals[j]
    late_ref[...] = jnp.zeros_like(late_ref)
    place = lax.broadcasted_iota(jnp.int32, (RIM, lanes), 0)
    for j in range(count):
        lag = lags[j]
        last = extra_ref[j, hours - RIM :]
        after = pltpu.roll(scan_rows(last, True)[0] - last, lag, 0)
        late_ref[sinks[j]] = late_ref[sinks[j]] - jnp.where(place < lag, after, 0.0)
    for i in range(count):
        at = slice(EDGE * i, EDGE * (i + 1))
        minerim_ref[at] = late_ref[i, 0:EDGE]
        theirsrim_ref[at] = late_ref[count + i, 0:EDGE]
    for i in range(2 * count):
        change = tot[i]
        if i < count:
            change = change + (stock_ref[i, hours - 1 : hours] - totals[i])
        tots_ref[i : i + 1] = change
    power_ref[...] = power


def windows_kernel(down_ref, delay_ref, extra_ref, stock_ref, new_ref, new_hbm, mine_ref, theirs_ref, sem):
    copy = pltpu.make_async_copy(new_ref, new_hbm, sem)
    copy.start()
    count, hours, lanes = extra_ref.shape
    sinks, lags = routes(down_ref, delay_ref)
    mine_ref[...] = jnp.zeros_like(mine_ref)
    theirs_ref[...] = jnp.zeros_like(theirs_ref)
    place = lax.broadcasted_iota(jnp.int32, (RIM, lanes), 0)
    zeros = jnp.zeros((RIM, lanes), jnp.float32)
    for j in range(count):
        sums, _ = scan_rows(extra_ref[j], False)
        arrived = place >= lags[j]
        tiles = [zeros] + turned([sums[k : k + RIM] for k in range(0, hours, RIM)], lags[j])
        window = jnp.concatenate([jnp.where(arrived, tiles[k + 1], tiles[k]) for k in range(hours // RIM)], 0)

        @pl.when(sinks[j] < count)
        def _():
            at = pl.ds(pl.multiple_of(sinks[j] * hours, RIM), hours)
            mine_ref[at] = mine_ref[at] + window

        @pl.when((sinks[j] >= count) & (sinks[j] < 2 * count))
        def _():
            at = pl.ds(pl.multiple_of((sinks[j] - count) * hours, RIM), hours)
            theirs_ref[at] = theirs_ref[at] + window

        at = slice(j * hours, (j + 1) * hours)
        mine_ref[at] = mine_ref[at] + (stock_ref[j] - sums)
    copy.wait()


def storage_kernel(scale_time, rows_ref, mine_ref, came_ref, rim_ref, off_ref, sd_ref, power_ref, dual_ref, demand_ref, sd_hbm, excess_hbm, dual_hbm, sd_out, excess_out, dual_out, sems, dual_sem):
    count, hours, lanes = sd_ref.shape
    earlier = lax.axis_index("hours") > 0
    copies = [[pltpu.make_async_copy(src.at[i], dst.at[i], sems.at[k, i]) for i in range(count)] for k, (src, dst) in enumerate(((sd_out, sd_hbm), (excess_out, excess_hbm)))]
    dual_out[...] = jnp.minimum(dual_ref[...] + dual_step * (power_ref[...] - demand_ref[...]), 0.0)
    dual_copy = pltpu.make_async_copy(dual_out, dual_hbm, dual_sem)
    dual_copy.start()
    for i in range(count):
        row = [rows_ref[k * count + i : k * count + i + 1] for k in range(5)]
        level, low, high = row[2] + scale_time * off_ref[i : i + 1], row[3], row[4]
        low_dual, high_dual = dual_step * low, dual_step * high
        for k in range(0, hours, RIM):
            at = slice(i * hours + k, i * hours + k + RIM)
            change = mine_ref[at] + came_ref[at]
            if k == 0:
                rim = jnp.where(earlier, rim_ref[EDGE * i : EDGE * (i + 1)], 0.0)
                change = change + jnp.concatenate([rim, jnp.zeros((RIM - EDGE, lanes), jnp.float32)], 0)
            storage = level + scale_time * change
            ahead = sd_ref[i, k : k + RIM] + dual_step * storage
            sd_out[i, k : k + RIM] = ahead - jnp.clip(ahead, low_dual, high_dual)
            excess_out[i, k : k + RIM] = storage - jnp.clip(storage, low, high)
        copies[0][i].start()
        copies[1][i].start()
    for i in range(count):
        for k in range(2):
            copies[k][i].wait()
    dual_copy.wait()


def passed_along(block, axis, distance):
    count = lax.axis_size(axis)
    return lax.ppermute(block, axis, [(i, (i + distance) % count) for i in range(count)])


def swapped(block, axis, bit):
    return lax.ppermute(block, axis, [(i, i ^ bit) for i in range(lax.axis_size(axis))])


def all_summed(part, axis, done):
    for step in range(done, (lax.axis_size(axis) - 1).bit_length()):
        part = part + swapped(part, axis, 1 << step)
    return part


def offsets(total, axis, reverse, beside):
    count, place = lax.axis_size(axis), lax.axis_index(axis)
    result = jnp.zeros_like(total)
    for step in range((count - 1).bit_length()):
        bit = 1 << step
        other = swapped(total, axis, bit)
        if step < len(beside) and beside[step]:
            other, *_ = lax.optimization_barrier((other, *beside[step]))
        low = (place & bit) == 0
        result = result + jnp.where(low if reverse else ~low, other, 0.0)
        total = total + other
    return result


VMEM = pl.BlockSpec(memory_space=pltpu.VMEM)
HBM = pl.BlockSpec(memory_space=pltpu.HBM)


def call(body, ins, outs, scratch):
    return pl.pallas_call(
        body,
        out_shape=[jax.ShapeDtypeStruct(shape, jnp.float32) for _, shape in outs],
        in_specs=[spec for spec, _ in ins],
        out_specs=[spec for spec, _ in outs],
        scratch_shapes=[pltpu.VMEM(entry, jnp.float32) if isinstance(entry, tuple) else entry for entry in scratch],
        compiler_params=pltpu.CompilerParams(vmem_limit_bytes=32 * 1024 * 1024),
    )(*(array for _, array in ins))


def shards(
    release,
    storage_dual,
    demand_dual,
    cost,
    inflow,
    demand,
    storage_start,
    storage_low,
    storage_high,
    release_cap,
    efficiency,
    downstream,
    travel_delay,
):
    count, hours, lanes = release.shape
    scale_time = 1.0 / (hours * lax.axis_size("hours"))
    scale_sum = 1.0 / math.sqrt(count * lax.axis_size("river"))
    slab, flat = (count, hours, lanes), (count, lanes)
    wide, edges = (count * hours, lanes), (count * EDGE, lanes)
    dma = pltpu.SemaphoreType.DMA

    (total,) = call(totals_kernel, [(VMEM, storage_dual)], [(VMEM, flat)], [])
    (sd_sent,) = call(copy_kernel, [(VMEM, lax.optimization_barrier((storage_dual, total))[0])], [(VMEM, slab)], [])
    sd_next = passed_along(sd_sent, "river", -1)
    base, rows = call(
        functools.partial(price_kernel, scale_sum),
        [(VMEM, a) for a in (efficiency, release_cap, storage_start, storage_low, storage_high, release, cost, demand_dual)],
        [(VMEM, slab), (VMEM, (5 * count, lanes))],
        [],
    )
    (stock,) = call(stock_kernel, [(VMEM, inflow)], [(VMEM, slab)], [])
    lead, w_sent = call(
        route_kernel,
        [(VMEM, a) for a in (downstream, travel_delay, storage_dual, sd_next)],
        [(VMEM, slab), (VMEM, edges)],
        [(2 * count + 1, hours, lanes)],
    )
    w = passed_along(w_sent, "hours", -1)
    off_own = offsets(total, "hours", True, [(base, rows), (lead, w_sent, stock), (stock,)])
    off_next = passed_along(off_own, "river", -1)

    new, extra, rim_mine, rim_theirs, tots, power = call(
        functools.partial(release_kernel, scale_time, scale_sum),
        [(VMEM, a) for a in (downstream, travel_delay, rows, base, lead, w, off_own, off_next, release, stock)],
        [(VMEM, slab), (VMEM, slab), (VMEM, edges), (VMEM, edges), (VMEM, (2 * count, lanes)), (VMEM, (hours, lanes))],
        [(2 * count + 1, 1, lanes), (2 * count + 1, RIM, lanes)],
    )
    release_new, mine, theirs = call(
        windows_kernel,
        [(VMEM, a) for a in (downstream, travel_delay, extra, stock, new)],
        [(HBM, slab), (VMEM, wide), (VMEM, wide)],
        [dma],
    )

    tot_came = passed_along(tots[count:], "river", 1)
    power = power + swapped(power, "river", 1)
    pairs = lax.axis_size("river") == 4
    if pairs:
        moved = passed_along(jnp.concatenate([rim_theirs, power], 0), "river", 1)
        late = rim_mine + moved[: count * EDGE]
        whole = power + moved[count * EDGE :]
    else:
        late = rim_mine + passed_along(rim_theirs, "river", 1)
    tot_came, theirs, power = lax.optimization_barrier((tot_came, theirs, power))
    came = passed_along(theirs, "river", 1)
    edge = passed_along(late, "hours", 1)
    place, steps = lax.axis_index("hours"), (lax.axis_size("hours") - 1).bit_length()
    tot = tots[:count] + tot_came
    off = jnp.zeros_like(tot)
    for step in range(steps):
        other = swapped(tot, "hours", 1 << step)
        if step == 0:
            other, late = lax.optimization_barrier((other, late))
            if pairs:
                supplied = jnp.where(lax.axis_index("river") % 2 == 0, whole, swapped(whole, "river", 1))
            else:
                supplied = all_summed(power, "river", 1)
        if step == 1:
            other, came = lax.optimization_barrier((other, came))
        if step == steps - 1:
            other, edge = lax.optimization_barrier((other, edge))
        off = off + jnp.where((place & (1 << step)) != 0, other, 0.0)
        tot = tot + other
    storage_dual_new, storage_excess, demand_dual_new = call(
        functools.partial(storage_kernel, scale_time),
        [(VMEM, a) for a in (rows, mine, came, edge, off, storage_dual, supplied, demand_dual, demand)],
        [(HBM, slab), (HBM, slab), (HBM, (hours, lanes))],
        [slab, slab, (hours, lanes), dma((2, count)), dma],
    )
    return (release_new, storage_dual_new, demand_dual_new, storage_excess)


def solution(mesh):
    field, flat, row = P("river", "hours", None), P("hours", None), P("river")
    return jax.shard_map(
        shards,
        mesh=mesh,
        in_specs=(field, field, flat, field, field, flat) + (row,) * 7,
        out_specs=(field, field, flat, field),
        check_vma=False,
    )
```
